32 devices in a mesh: row: 4 (over y, x), col: 8 (over z, core).
Axes of the slice: x: 2, y: 2, z: 4, core: 2. Of those that a mesh axis runs over, the one named last changes fastest.
Arguments:
- points: float32 [8192, 64], P(('row', 'col')), may hold values from -6 to 6
- feature_scales: float32 [64], replicated, may hold values from 0.06 to 0.25
- amplitude: float32 [1], replicated, may hold values from 1 to 3
- ridge: float32 [1], replicated, may hold values from 0.5 to 2
Outputs:
- factored: float32 [12, 8, 16, 4, 2048], P(None, 'col', None, 'row')
The draws below stay inside these ranges and needn't reach their ends.
All inputs are finite; a program needn't handle non-finite values.
Results may differ from the reference program's by a relative error of at most 0.0009.
The reference program's roundings to bfloat16 on the way (of `center_first`, `center_panels`, `first_panel` and `second_panel`) count: a program that leaves them out, or rounds other values in their place, can miss the bound.
Values may be sent and summed in bfloat16 or wider, within the bound.
A program may use at most 128 MiB of HBM per device.

```python
import math
import jax
import jax.numpy as jnp
from jax import lax

FEAT = 64
SLAB = 1536
PANEL = 256
BLK = 16
NB = 64
NPTS = 8192
TB = 12
SB = 32
N_ROW = 4
N_COL = 8


def shard_levels(key, extent, pieces, smallest, high):
    gain = 1.0
    for axis_at, blocks in pieces:
        heights = jax.random.uniform(jax.random.fold_in(jax.random.fold_in(key, 6), axis_at), (blocks,), jnp.float32, smallest / len(pieces), high / len(pieces))
        gain = gain * jnp.repeat(jnp.exp(heights), extent[axis_at] // blocks).reshape((-1,) + (1,) * (len(extent) - 1 - axis_at))
    return gain


def noise(own_key, shape, deviation, limit, split=(), kind=jnp.bfloat16):
    entries = deviation * jax.random.normal(own_key, shape, jnp.float32)
    if split:
        entries = entries * shard_levels(own_key, shape, split, -0.22, 0.18)
    return jnp.clip(entries, -limit, limit).astype(kind)


def setup_inputs(seed: int = 0) -> dict:
    seeds = jax.random.split(jax.random.key(seed), 5)
    points = noise(seeds[0], (NPTS, FEAT), 1.0, 6.0, ((0, 32),), jnp.float32)
    feature_scales = jnp.clip(jnp.exp(jax.random.uniform(seeds[1], (FEAT,), jnp.float32, math.log(0.06), math.log(0.25))), 0.06, 0.25)
    amplitude = jnp.clip(jnp.exp(jax.random.uniform(seeds[2], (1,), jnp.float32, math.log(1.0), math.log(3.0))), 1.0, 3.0)
    ridge = jnp.clip(jnp.exp(jax.random.uniform(seeds[3], (1,), jnp.float32, math.log(0.5), math.log(2.0))), 0.5, 2.0)
    return dict(points=points, feature_scales=feature_scales, amplitude=amplitude, ridge=ridge)


def kernel_rows(left, right, scales, signal):
    left_scaled = left * scales
    right_scaled = right * scales
    left_norms = jnp.sum(left_scaled * left_scaled, axis=1)
    right_norms = jnp.sum(right_scaled * right_scaled, axis=1)
    cross = jnp.dot(left_scaled.astype(jnp.float32), right_scaled.T.astype(jnp.float32), precision=lax.Precision.HIGHEST, preferred_element_type=jnp.float32)
    return signal * jnp.exp(-0.5 * (left_norms[:, None] + right_norms[None, :] - 2.0 * cross))

def lower_inverse(block):
    factor = jnp.linalg.cholesky(block)
    identity = jnp.eye(block.shape[0], dtype=jnp.float32)
    return lax.linalg.triangular_solve(factor, identity, left_side=True, lower=True)

def factor_centers(centers, scales, signal, jitter):
    center_kernel = kernel_rows(centers, centers, scales, signal) + jitter * jnp.eye(centers.shape[0], dtype=jnp.float32)
    first_inverse = lower_inverse(center_kernel[:PANEL, :PANEL])
    center_first = jnp.dot(center_kernel[:, :PANEL].astype(jnp.float32), first_inverse.T.astype(jnp.float32), precision=lax.Precision.HIGHEST, preferred_element_type=jnp.float32).astype(jnp.bfloat16)
    center_second = center_kernel[:, PANEL:2 * PANEL] - jnp.dot(center_first.astype(jnp.float32), center_first[PANEL:2 * PANEL].T.astype(jnp.float32), preferred_element_type=jnp.float32)
    second_inverse = lower_inverse(center_second[PANEL:2 * PANEL])
    second_part = jnp.dot(center_second.astype(jnp.float32), second_inverse.T.astype(jnp.float32), precision=lax.Precision.HIGHEST, preferred_element_type=jnp.float32).astype(jnp.bfloat16)
    return (first_inverse, second_inverse, jnp.concatenate([center_first, second_part], axis=1))

def reference(points, feature_scales, amplitude, ridge):
    signal = amplitude[0]
    jitter = ridge[0]
    centers = points[:SLAB]
    first_inverse, second_inverse, center_panels = factor_centers(centers, feature_scales, signal, jitter)
    slab = kernel_rows(centers, points, feature_scales, signal)
    slab = slab.at[:, :SLAB].add(jitter * jnp.eye(SLAB, dtype=jnp.float32))
    first_panel = jnp.dot(first_inverse.astype(jnp.float32), slab[:PANEL].astype(jnp.float32), precision=lax.Precision.HIGHEST, preferred_element_type=jnp.float32).astype(jnp.bfloat16)
    reduced = slab[PANEL:2 * PANEL] - jnp.dot(center_panels[PANEL:2 * PANEL, :PANEL].astype(jnp.float32), first_panel.astype(jnp.float32), preferred_element_type=jnp.float32)
    second_panel = jnp.dot(second_inverse.astype(jnp.float32), reduced.astype(jnp.float32), precision=lax.Precision.HIGHEST, preferred_element_type=jnp.float32).astype(jnp.bfloat16)
    both_panels = jnp.concatenate([first_panel, second_panel], axis=0)
    trailing = slab[2 * PANEL:] - jnp.dot(center_panels[2 * PANEL:].astype(jnp.float32), both_panels.astype(jnp.float32), preferred_element_type=jnp.float32)
    factored = jnp.concatenate([both_panels.astype(jnp.float32), trailing], axis=0)
    factored = factored.reshape(TB, N_COL, BLK, SB, N_ROW, NB).transpose(0, 1, 2, 4, 3, 5)
    return factored.reshape(TB, N_COL, BLK, N_ROW, SB * NB)
```

```python
import functools

import jax
import jax.numpy as jnp
from jax import lax
from jax.experimental import pallas as pl
from jax.experimental.pallas import tpu as pltpu
from jax.sharding import PartitionSpec as P

FEAT = 64
SLAB = 1536
PANEL = 256
BLK = 16
BASE = 64
SUB = 8
HIGHEST = lax.Precision.HIGHEST
MESH = pl.DeviceIdType.MESH


def pack(rows):
    half = rows.shape[-2] // 2
    return jnp.concatenate([rows[..., :half, :], rows[..., half:, :]], axis=-1)


def unpack(rows):
    return jnp.concatenate([rows[..., :FEAT], rows[..., FEAT:]], axis=-2)


def exchange_kernel(
    n_row, n_col, n_panel, n_trail,
    blocks, strips, rows_out, panel_out, trail_out,
    send_sem, recv_sem, trail_send, trail_recv, panel_send, panel_recv, local_sem,
):
    n_dev = n_row * n_col
    my_row = lax.axis_index("row")
    my_col = lax.axis_index("col")
    me = my_row * n_col + my_col
    has_trail = jnp.logical_and(me >= n_panel, me < n_panel + n_trail)

    def place(step):
        peer = lax.rem(me + step, n_dev)
        return peer, lax.div(peer, n_col), lax.rem(peer, n_col)

    barrier = pltpu.get_barrier_semaphore()

    @pl.loop(1, n_dev)
    def _(step):
        _, row, col = place(step)
        pl.semaphore_signal(barrier, inc=1, device_id=(row, col), device_id_type=MESH)

    pl.semaphore_wait(barrier, n_dev - 1)

    def block_copy(step):
        _, row, col = place(step)
        return pltpu.make_async_remote_copy(
            src_ref=blocks.at[row], dst_ref=rows_out.at[me],
            send_sem=send_sem.at[step], recv_sem=recv_sem.at[me],
            device_id=(row, col), device_id_type=MESH,
        )

    def trail_copy(step):
        _, row, col = place(step)
        return pltpu.make_async_remote_copy(
            src_ref=strips.at[:, col], dst_ref=trail_out.at[me - n_panel],
            send_sem=trail_send.at[step], recv_sem=trail_recv.at[me - n_panel],
            device_id=(row, col), device_id_type=MESH,
        )

    def panel_copy(source, step):
        row = lax.rem(my_row + step, n_row)
        return pltpu.make_async_remote_copy(
            src_ref=rows_out.at[source], dst_ref=panel_out.at[source, my_row],
            send_sem=panel_send.at[source, step], recv_sem=panel_recv.at[source, my_row],
            device_id=(row, my_col), device_id_type=MESH,
        )

    def arrival(source):
        return pltpu.make_async_remote_copy(
            src_ref=blocks.at[0], dst_ref=rows_out.at[source],
            send_sem=send_sem.at[0], recv_sem=recv_sem.at[source],
            device_id=(my_row, my_col), device_id_type=MESH,
        )

    @pl.loop(1, n_dev)
    def _(step):
        block_copy(step).start()

    own = pltpu.make_async_copy(blocks.at[my_row], rows_out.at[me], local_sem.at[0])
    own.start()
    own.wait()

    @pl.when(has_trail)
    def _():
        @pl.loop(1, n_dev)
        def _(step):
            trail_copy(step).start()

        kept = pltpu.make_async_copy(
            strips.at[:, my_col], trail_out.at[me - n_panel], local_sem.at[0]
        )
        kept.start()
        kept.wait()

    for source in range(n_panel):
        @pl.when(me != source)
        def _():
            arrival(source).wait_recv()

        kept = pltpu.make_async_copy(
            rows_out.at[source], panel_out.at[source, my_row], local_sem.at[0]
        )
        kept.start()
        for step in range(1, n_row):
            panel_copy(source, step).start()
        kept.wait()

    @pl.loop(n_panel, n_dev)
    def _(source):
        @pl.when(me != source)
        def _():
            arrival(source).wait_recv()

    @pl.loop(0, n_trail)
    def _(source):
        @pl.when(me != source + n_panel)
        def _():
            pltpu.make_async_remote_copy(
                src_ref=strips.at[:, my_col], dst_ref=trail_out.at[source],
                send_sem=trail_send.at[0], recv_sem=trail_recv.at[source],
                device_id=(my_row, my_col), device_id_type=MESH,
            ).wait_recv()

    for source in range(n_panel):
        for step in range(1, n_row):
            row = lax.rem(my_row + step, n_row)
            pltpu.make_async_remote_copy(
                src_ref=rows_out.at[source], dst_ref=panel_out.at[source, row],
                send_sem=panel_send.at[source, 0], recv_sem=panel_recv.at[source, row],
                device_id=(my_row, my_col), device_id_type=MESH,
            ).wait_recv()
            panel_copy(source, step).wait_send()

    @pl.loop(1, n_dev)
    def _(step):
        block_copy(step).wait_send()

    @pl.when(has_trail)
    def _():
        @pl.loop(1, n_dev)
        def _(step):
            trail_copy(step).wait_send()


def exchange(points, n_row, n_col):
    rows_one = points.shape[0]
    n_dev = n_row * n_col
    block_rows = rows_one // n_row
    n_panel = 2 * PANEL // rows_one
    n_trail = SLAB // rows_one - n_panel
    strips_one = rows_one // (BLK * n_col)
    blocks = pack(points.reshape(n_row, block_rows, FEAT))
    strips = pack(points.reshape(strips_one, n_col, BLK, FEAT))
    piece = (block_rows // 2, 2 * FEAT)
    vmem = pl.BlockSpec(memory_space=pltpu.VMEM)
    rows, panel, trail = pl.pallas_call(
        functools.partial(exchange_kernel, n_row, n_col, n_panel, n_trail),
        out_shape=(
            jax.ShapeDtypeStruct((n_dev, *piece), jnp.float32),
            jax.ShapeDtypeStruct((n_panel, n_row, *piece), jnp.float32),
            jax.ShapeDtypeStruct((n_trail, strips_one, BLK // 2, 2 * FEAT), jnp.float32),
        ),
        in_specs=[vmem] * 2,
        out_specs=(vmem,) * 3,
        scratch_shapes=[
            pltpu.SemaphoreType.DMA((n_dev,)),
            pltpu.SemaphoreType.DMA((n_dev,)),
            pltpu.SemaphoreType.DMA((n_dev,)),
            pltpu.SemaphoreType.DMA((n_trail,)),
            pltpu.SemaphoreType.DMA((n_panel, n_row)),
            pltpu.SemaphoreType.DMA((n_panel, n_row)),
            pltpu.SemaphoreType.DMA((1,)),
        ],
        compiler_params=pltpu.CompilerParams(collective_id=0, has_side_effects=True),
    )(blocks, strips)
    return (
        unpack(rows).reshape(-1, FEAT),
        unpack(panel).reshape(-1, FEAT),
        unpack(trail).reshape(-1, FEAT),
    )


def base_inverse(block):
    row = lax.broadcasted_iota(jnp.int32, (BASE, BASE), 0)
    col = lax.broadcasted_iota(jnp.int32, (BASE, BASE), 1)
    both = jnp.concatenate([block, (row == col).astype(jnp.float32)], axis=1)
    groups = BASE // SUB
    full = (SUB, 2 * BASE)
    rows = [both[SUB * g : SUB * (g + 1)] for g in range(groups)]
    inside = lax.broadcasted_iota(jnp.int32, full, 0)
    for g in range(groups):
        cols = [
            {b: jnp.broadcast_to(rows[b][:, SUB * g + j : SUB * g + j + 1], full) for b in range(g, groups)}
            for j in range(SUB)
        ]
        scale = jnp.zeros(full, jnp.float32)
        for j in range(SUB):
            own = cols[j][g]
            pivot = jnp.broadcast_to(own[j : j + 1], full)
            inverse = 1.0 / pivot
            scale = jnp.where(inside == j, lax.rsqrt(pivot), scale)
            lead = jnp.broadcast_to(rows[g][j : j + 1], full) * inverse
            factors = dict(cols[j])
            factors[g] = jnp.where(inside > j, own, 0.0)
            for k in range(j + 1, SUB):
                weight = jnp.broadcast_to(own[k : k + 1], full) * inverse
                for b in range(g, groups):
                    cols[k][b] = cols[k][b] - factors[b] * weight
            for b in range(g, groups):
                rows[b] = rows[b] - factors[b] * lead
        rows[g] = rows[g] * scale
    return jnp.concatenate([r[:, BASE:] for r in rows], axis=0)


def full_dot(a, b, dims=((1,), (0,))):
    return lax.dot_general(
        a, b, (dims, ((), ())), precision=HIGHEST, preferred_element_type=jnp.float32
    )


def inverse_factor(a, out_ref, work):
    work[:, :PANEL] = (a + a.T) * 0.5
    row = lax.broadcasted_iota(jnp.int32, (PANEL, PANEL), 0)
    col = lax.broadcasted_iota(jnp.int32, (PANEL, PANEL), 1)
    work[:, PANEL:] = (row == col).astype(jnp.float32)
    lane = lax.broadcasted_iota(jnp.int32, (BASE, PANEL), 1)

    @pl.loop(0, PANEL // BASE)
    def _(step):
        start = pl.multiple_of(step * BASE, BASE)
        strip = work[pl.ds(start, BASE), :]
        turned = pltpu.roll(strip[:, :PANEL], lax.rem(PANEL - start, PANEL), 1)
        inverse = base_inverse(turned[:, :BASE])
        solved = full_dot(inverse, strip)
        below = jnp.where(lane >= start + BASE, solved[:, :PANEL], 0.0)
        work[...] = work[...] - full_dot(below, solved, ((0,), (0,)))
        out_ref[pl.ds(start, BASE), :] = solved[:, PANEL:]


def inverse_kernel(a_ref, out_ref, work):
    inverse_factor(a_ref[...], out_ref, work)


def lower_inverse(block):
    return pl.pallas_call(
        inverse_kernel,
        out_shape=jax.ShapeDtypeStruct((PANEL, PANEL), jnp.float32),
        in_specs=[pl.BlockSpec(memory_space=pltpu.VMEM)],
        out_specs=pl.BlockSpec(memory_space=pltpu.VMEM),
        scratch_shapes=[pltpu.VMEM((PANEL, 2 * PANEL), jnp.float32)],
        compiler_params=pltpu.CompilerParams(vmem_limit_bytes=32 * 1024 * 1024),
    )(block)


def kernel_rows(left, right, scales, signal):
    left_scaled = left * scales
    right_scaled = right * scales
    left_norms = jnp.sum(left_scaled * left_scaled, axis=1)
    right_norms = jnp.sum(right_scaled * right_scaled, axis=1)
    cross = jnp.dot(
        left_scaled, right_scaled.T, precision=HIGHEST, preferred_element_type=jnp.float32
    )
    return signal * jnp.exp(-0.5 * (left_norms[:, None] + right_norms[None, :] - 2.0 * cross))


def on_device(points, feature_scales, amplitude, ridge):
    n_row = lax.axis_size("row")
    n_col = lax.axis_size("col")
    block_rows = points.shape[0] // n_row
    n_points = points.shape[0] * n_col
    col_blocks = SLAB // (BLK * n_col)
    panel_blocks = PANEL // (BLK * n_col)
    signal = amplitude[0]
    jitter = ridge[0]
    process_row = lax.axis_index("row")
    column = lax.axis_index("col")
    row_points, panel_centers, own_centers = exchange(points, n_row, n_col)
    chosen = jnp.concatenate([panel_centers, own_centers], axis=0)

    center = kernel_rows(chosen, panel_centers, feature_scales, signal)
    center = center + jitter * jnp.eye(chosen.shape[0], 2 * PANEL, dtype=jnp.float32)
    first_inverse = lower_inverse(center[:PANEL, :PANEL])
    center_first = jnp.dot(
        center[PANEL:, :PANEL], first_inverse.T, precision=HIGHEST, preferred_element_type=jnp.float32
    ).astype(jnp.bfloat16)
    center_second = center[PANEL:, PANEL:] - jnp.dot(
        center_first, center_first[:PANEL].T, preferred_element_type=jnp.float32
    )
    second_inverse = lower_inverse(center_second[:PANEL])
    second_part = jnp.dot(
        center_second[PANEL:], second_inverse.T, precision=HIGHEST, preferred_element_type=jnp.float32
    ).astype(jnp.bfloat16)
    own_table = jnp.concatenate([center_first[PANEL:], second_part], axis=1)

    kernel = kernel_rows(chosen, row_points, feature_scales, signal)
    shape = kernel.shape
    trail = col_blocks - 2 * panel_blocks
    owned = (
        (lax.broadcasted_iota(jnp.int32, (trail, BLK), 0) + 2 * panel_blocks) * n_col + column
    ) * BLK + lax.broadcasted_iota(jnp.int32, (trail, BLK), 1)
    col_index = jnp.concatenate(
        [lax.broadcasted_iota(jnp.int32, (2 * PANEL,), 0), owned.reshape(-1)]
    )[:, None]
    grid_pos = lax.broadcasted_iota(jnp.int32, shape, 1)
    row_index = (grid_pos // block_rows * n_row + process_row) * block_rows + grid_pos % block_rows
    kernel = kernel + jnp.where(col_index == row_index, jitter, jnp.float32(0.0))
    first_panel = jnp.dot(
        first_inverse, kernel[:PANEL], precision=HIGHEST, preferred_element_type=jnp.float32
    ).astype(jnp.bfloat16)
    adjusted = kernel[PANEL : 2 * PANEL] - jnp.dot(
        center_first[:PANEL], first_panel, preferred_element_type=jnp.float32
    )
    second_panel = jnp.dot(
        second_inverse, adjusted, precision=HIGHEST, preferred_element_type=jnp.float32
    ).astype(jnp.bfloat16)
    both_panels = jnp.concatenate([first_panel, second_panel], axis=0)
    trailing = kernel[2 * PANEL :] - jnp.dot(
        own_table, both_panels, preferred_element_type=jnp.float32
    )
    own_panels = lax.dynamic_index_in_dim(
        both_panels.reshape(2 * panel_blocks, n_col, BLK, n_points), column, 1, False
    ).astype(jnp.float32)
    finished = jnp.concatenate([own_panels, trailing.reshape(trail, BLK, n_points)], axis=0)
    return finished.reshape(col_blocks, 1, BLK, 1, n_points)


def solution(mesh):
    placed = (P(("row", "col"), None), P(), P(), P())
    return jax.shard_map(
        on_device,
        mesh=mesh,
        in_specs=placed,
        out_specs=P(None, "col", None, "row", None),
        check_vma=False,
    )
```

```python
import functools

import jax
import jax.numpy as jnp
from jax import lax
from jax.experimental import pallas as pl
from jax.experimental.pallas import tpu as pltpu
from jax.sharding import PartitionSpec as P

FEAT = 64
SLAB = 1536
PANEL = 256
BLK = 16
BASE = 64
SUB = 8
HIGHEST = lax.Precision.HIGHEST
MESH = pl.DeviceIdType.MESH


def pack(rows):
    half = rows.shape[-2] // 2
    return jnp.concatenate([rows[..., :half, :], rows[..., half:, :]], axis=-1)


def unpack(rows):
    return jnp.concatenate([rows[..., :FEAT], rows[..., FEAT:]], axis=-2)


def split(x):
    high = x.astype(jnp.bfloat16)
    rest = x - high.astype(jnp.float32)
    middle = rest.astype(jnp.bfloat16)
    low = (rest - middle.astype(jnp.float32)).astype(jnp.bfloat16)
    return high, middle, low


def joined_dot(a, b, dims):
    ah, am, al = split(a)
    bh, bm, bl = split(b)
    left = jnp.concatenate([ah, ah, am, ah, al, am], axis=dims[0][0])
    right = jnp.concatenate([bh, bm, bh, bl, bh, bm], axis=dims[1][0])
    return lax.dot_general(left, right, (dims, ((), ())), preferred_element_type=jnp.float32)


def gaussian(left, right, signal):
    left_norms = 0.5 * jnp.sum(left * left, axis=1, keepdims=True)
    right_norms = full_dot(jnp.full((8, FEAT), 0.5, jnp.float32), right * right, ((1,), (1,)))[:1]
    cross = joined_dot(left, right, ((1,), (1,)))
    return signal * jnp.exp(cross - left_norms - right_norms)


def factor_kernel(
    n_row, n_col, n_panel, n_trail,
    numbers, points, scales,
    rows_out, panel_out, trail_out, inverse_one, inverse_two, second_rows, own_table,
    blocks, strips, work_a, work_x,
    send_sem, recv_sem, trail_send, trail_recv, panel_send, panel_recv, local_sem,
):
    n_dev = n_row * n_col
    my_row = lax.axis_index("row")
    my_col = lax.axis_index("col")
    me = my_row * n_col + my_col
    has_trail = jnp.logical_and(me >= n_panel, me < n_panel + n_trail)
    has_panel = me < n_panel
    values = points[...]
    blocks[...] = pack(values.reshape(blocks.shape[0], -1, FEAT))
    strips[...] = pack(values.reshape(strips.shape[0], strips.shape[1], BLK, FEAT))

    def place(step):
        peer = lax.rem(me + step, n_dev)
        return peer, lax.div(peer, n_col), lax.rem(peer, n_col)

    barrier = pltpu.get_barrier_semaphore()

    @pl.loop(1, n_dev)
    def _(step):
        _, row, col = place(step)
        pl.semaphore_signal(barrier, inc=1, device_id=(row, col), device_id_type=MESH)

    pl.semaphore_wait(barrier, n_dev - 1)

    def block_copy(step):
        _, row, col = place(step)
        return pltpu.make_async_remote_copy(
            src_ref=blocks.at[row], dst_ref=rows_out.at[me],
            send_sem=send_sem.at[step], recv_sem=recv_sem.at[me],
            device_id=(row, col), device_id_type=MESH,
        )

    def trail_copy(step):
        _, row, col = place(step)
        return pltpu.make_async_remote_copy(
            src_ref=strips.at[:, col], dst_ref=trail_out.at[me - n_panel],
            send_sem=trail_send.at[step], recv_sem=trail_recv.at[me - n_panel],
            device_id=(row, col), device_id_type=MESH,
        )

    def panel_copy(source, step):
        row = lax.rem(my_row + step, n_row)
        return pltpu.make_async_remote_copy(
            src_ref=rows_out.at[source], dst_ref=panel_out.at[source, my_row],
            send_sem=panel_send.at[source, step], recv_sem=panel_recv.at[source, my_row],
            device_id=(row, my_col), device_id_type=MESH,
        )

    def arrival(source):
        return pltpu.make_async_remote_copy(
            src_ref=blocks.at[0], dst_ref=rows_out.at[source],
            send_sem=send_sem.at[0], recv_sem=recv_sem.at[source],
            device_id=(my_row, my_col), device_id_type=MESH,
        )

    def send_blocks():
        @pl.loop(1, n_dev)
        def _(step):
            block_copy(step).start()

    pl.when(has_panel)(send_blocks)

    own = pltpu.make_async_copy(blocks.at[my_row], rows_out.at[me], local_sem.at[0])
    own.start()
    own.wait()

    for source in range(n_panel):
        @pl.when(me != source)
        def _():
            arrival(source).wait_recv()

        kept = pltpu.make_async_copy(
            rows_out.at[source], panel_out.at[source, my_row], local_sem.at[0]
        )
        kept.start()
        for step in range(1, n_row):
            panel_copy(source, step).start()
        kept.wait()

    @pl.when(has_trail)
    def _():
        @pl.loop(1, n_dev)
        def _(step):
            trail_copy(step).start()

        kept = pltpu.make_async_copy(
            strips.at[:, my_col], trail_out.at[me - n_panel], local_sem.at[0]
        )
        kept.start()
        kept.wait()

    pl.when(jnp.logical_not(has_panel))(send_blocks)

    for source in range(n_panel):
        for step in range(1, n_row):
            row = lax.rem(my_row + step, n_row)
            pltpu.make_async_remote_copy(
                src_ref=rows_out.at[source], dst_ref=panel_out.at[source, row],
                send_sem=panel_send.at[source, 0], recv_sem=panel_recv.at[source, row],
                device_id=(my_row, my_col), device_id_type=MESH,
            ).wait_recv()
            panel_copy(source, step).wait_send()

    signal = numbers[0]
    jitter = numbers[1]
    scale = scales[...]
    panel = unpack(panel_out[...]).reshape(2 * PANEL, FEAT) * scale
    center = gaussian(panel, panel, signal)
    row = lax.broadcasted_iota(jnp.int32, center.shape, 0)
    col = lax.broadcasted_iota(jnp.int32, center.shape, 1)
    center = center + jnp.where(row == col, jitter, 0.0)
    inverse_factor(center[:PANEL, :PANEL], inverse_one, work_a, work_x)
    low_first = full_dot(center[PANEL:, :PANEL], inverse_one[...], ((1,), (1,))).astype(jnp.bfloat16)
    second_rows[...] = low_first
    low_second = center[PANEL:, PANEL:] - plain_dot(low_first, low_first, ((1,), (1,)))
    inverse_factor(low_second, inverse_two, work_a, work_x)

    @pl.loop(0, n_trail)
    def _(source):
        @pl.when(me != source + n_panel)
        def _():
            pltpu.make_async_remote_copy(
                src_ref=strips.at[:, my_col], dst_ref=trail_out.at[source],
                send_sem=trail_send.at[0], recv_sem=trail_recv.at[source],
                device_id=(my_row, my_col), device_id_type=MESH,
            ).wait_recv()

    owned = unpack(trail_out[...]).reshape(-1, FEAT) * scale
    own = gaussian(owned, panel, signal)
    own_first = full_dot(own[:, :PANEL], inverse_one[...], ((1,), (1,))).astype(jnp.bfloat16)
    own_second = own[:, PANEL:] - plain_dot(own_first, low_first, ((1,), (1,)))
    own_table[:, :PANEL] = own_first
    own_table[:, PANEL:] = full_dot(own_second, inverse_two[...], ((1,), (1,))).astype(jnp.bfloat16)

    @pl.loop(n_panel, n_dev)
    def _(source):
        @pl.when(me != source)
        def _():
            arrival(source).wait_recv()

    @pl.loop(1, n_dev)
    def _(step):
        block_copy(step).wait_send()

    @pl.when(has_trail)
    def _():
        @pl.loop(1, n_dev)
        def _(step):
            trail_copy(step).wait_send()


def exchange_and_factor(numbers, points, scales, n_row, n_col):
    rows_one = points.shape[0]
    n_dev = n_row * n_col
    n_panel = 2 * PANEL // rows_one
    n_trail = SLAB // rows_one - n_panel
    strips_one = rows_one // (BLK * n_col)
    piece = (rows_one // n_row // 2, 2 * FEAT)
    strip = (BLK // 2, 2 * FEAT)
    n_own = n_trail * strips_one * BLK
    vmem = pl.BlockSpec(memory_space=pltpu.VMEM)
    shape = jax.ShapeDtypeStruct
    return pl.pallas_call(
        functools.partial(factor_kernel, n_row, n_col, n_panel, n_trail),
        out_shape=(
            shape((n_dev, *piece), jnp.float32),
            shape((n_panel, n_row, *piece), jnp.float32),
            shape((n_trail, strips_one, *strip), jnp.float32),
            shape((PANEL, PANEL), jnp.float32),
            shape((PANEL, PANEL), jnp.float32),
            shape((PANEL, PANEL), jnp.bfloat16),
            shape((n_own, 2 * PANEL), jnp.bfloat16),
        ),
        in_specs=[pl.BlockSpec(memory_space=pltpu.SMEM), vmem, vmem],
        out_specs=(vmem,) * 7,
        scratch_shapes=[
            pltpu.VMEM((n_row, *piece), jnp.float32),
            pltpu.VMEM((strips_one, n_col, *strip), jnp.float32),
            pltpu.VMEM((PANEL, PANEL), jnp.float32),
            pltpu.VMEM((PANEL, PANEL), jnp.float32),
            pltpu.SemaphoreType.DMA((n_dev,)),
            pltpu.SemaphoreType.DMA((n_dev,)),
            pltpu.SemaphoreType.DMA((n_dev,)),
            pltpu.SemaphoreType.DMA((n_trail,)),
            pltpu.SemaphoreType.DMA((n_panel, n_row)),
            pltpu.SemaphoreType.DMA((n_panel, n_row)),
            pltpu.SemaphoreType.DMA((1,)),
        ],
        compiler_params=pltpu.CompilerParams(
            collective_id=0, has_side_effects=True, vmem_limit_bytes=40 * 1024 * 1024
        ),
    )(numbers, points, scales)


def base_inverse(block):
    row = lax.broadcasted_iota(jnp.int32, (BASE, BASE), 0)
    col = lax.broadcasted_iota(jnp.int32, (BASE, BASE), 1)
    both = jnp.concatenate([block, (row == col).astype(jnp.float32)], axis=1)
    groups = BASE // SUB
    done = []
    for g in range(groups):
        height = BASE - SUB * g
        shape = (height, 2 * BASE)
        inside = lax.broadcasted_iota(jnp.int32, shape, 0)
        cols = [jnp.broadcast_to(both[:, SUB * g + j : SUB * g + j + 1], shape) for j in range(SUB)]
        scale = jnp.zeros((SUB, BASE), jnp.float32)
        for j in range(SUB):
            pivot = cols[j][j : j + 1]
            inverse = 1.0 / pivot
            scale = jnp.where(inside[:SUB, :BASE] == j, lax.rsqrt(pivot[:, :BASE]), scale)
            factors = jnp.where(inside > j, cols[j], 0.0)
            for k in range(j + 1, SUB):
                cols[k] = cols[k] - factors * (cols[j][k : k + 1] * inverse)
            both = both - factors * (both[j : j + 1] * inverse)
        done.append(both[:SUB, BASE:] * scale)
        both = both[SUB:]
    return jnp.concatenate(done, axis=0)


def full_dot(a, b, dims=((1,), (0,))):
    return lax.dot_general(
        a, b, (dims, ((), ())), precision=HIGHEST, preferred_element_type=jnp.float32
    )


def plain_dot(a, b, dims=((1,), (0,))):
    return lax.dot_general(a, b, (dims, ((), ())), preferred_element_type=jnp.float32)


def inverse_factor(a, out_ref, work_a, work_x):
    work_a[...] = (a + a.T) * 0.5
    row = lax.broadcasted_iota(jnp.int32, (PANEL, PANEL), 0)
    col = lax.broadcasted_iota(jnp.int32, (PANEL, PANEL), 1)
    work_x[...] = (row == col).astype(jnp.float32)
    out_ref[...] = jnp.zeros((PANEL, PANEL), jnp.float32)
    for start in range(0, PANEL, BASE):
        stop = start + BASE
        first = start // 128 * 128
        last = (stop + 127) // 128 * 128
        inverse = base_inverse(work_a[start:stop, start:stop])
        solved_x = joined_dot(inverse, work_x[start:stop, :last], ((1,), (0,)))
        out_ref[start:stop, :last] = solved_x
        if stop == PANEL:
            break
        solved_a = joined_dot(inverse, work_a[start:stop, first:], ((1,), (0,)))
        below = solved_a[:, stop - first :]
        kept = stop // 128 * 128
        work_a[stop:, kept:] -= joined_dot(below, solved_a[:, kept - first :], ((0,), (0,)))
        work_x[stop:, :last] -= joined_dot(below, solved_x, ((0,), (0,)))


def slab_kernel(
    n_row, n_col, block_rows,
    numbers, position, panel_ref, trail_ref, scales, one_ref, two_ref, second_ref, table_ref, rows_ref,
    out_ref, keep_one, keep_two, chosen_ref,
):
    signal = numbers[0]
    jitter = numbers[1]
    process_row = position[0]
    column = position[1]
    scale = scales[...]

    @pl.when(pl.program_id(0) == 0)
    def _():
        chosen_ref[: 2 * PANEL] = unpack(panel_ref[...]).reshape(2 * PANEL, FEAT) * scale
        chosen_ref[2 * PANEL :] = unpack(trail_ref[...]).reshape(-1, FEAT) * scale

    chunk = rows_ref.shape[0] * block_rows
    points = unpack(rows_ref[...]).reshape(chunk, FEAT) * scale
    kernel = gaussian(chosen_ref[...], points, signal)
    shape = kernel.shape
    group = BLK * n_col
    col = lax.broadcasted_iota(jnp.int32, (shape[0], 1), 0)
    extra = col - 2 * PANEL
    owned = 2 * PANEL + extra // BLK * group + column * BLK + extra % BLK
    col = jnp.where(extra >= 0, owned, col)
    place = pl.program_id(0) * chunk + lax.broadcasted_iota(jnp.int32, (1, chunk), 1)
    row = (place // block_rows * n_row + process_row) * block_rows + place % block_rows
    kernel = kernel + jnp.where(col == row, jitter, 0.0)
    first = full_dot(one_ref[...], kernel[:PANEL]).astype(jnp.bfloat16)
    reduced = kernel[PANEL : 2 * PANEL] - plain_dot(second_ref[...], first)
    second = full_dot(two_ref[...], reduced).astype(jnp.bfloat16)
    trailing = kernel[2 * PANEL :] - (
        plain_dot(table_ref[:, :PANEL], first) + plain_dot(table_ref[:, PANEL:], second)
    )
    keep_one[...] = first.astype(jnp.float32)
    keep_two[...] = second.astype(jnp.float32)
    blocks = PANEL // group
    for which, keep in enumerate((keep_one, keep_two)):
        for t in range(blocks):
            start = pl.multiple_of(t * group + column * BLK, BLK)
            at = (which * blocks + t) * BLK
            out_ref[at : at + BLK] = keep[pl.ds(start, BLK), :].reshape(BLK, 1, chunk)
    out_ref[2 * blocks * BLK :] = trailing.reshape(trailing.shape[0], 1, chunk)


def slab(numbers, position, factored, scales, n_row, n_col, block_rows):
    rows, panel, trail, one, two, second, table = factored
    n_dev = n_row * n_col
    together = 512 // block_rows
    chunk = together * block_rows
    n_own = table.shape[0]
    n_out = n_own + 2 * PANEL // n_col
    vmem = pl.BlockSpec(memory_space=pltpu.VMEM)
    smem = pl.BlockSpec(memory_space=pltpu.SMEM)
    return pl.pallas_call(
        functools.partial(slab_kernel, n_row, n_col, block_rows),
        grid=(n_dev // together,),
        out_shape=jax.ShapeDtypeStruct((n_out, 1, n_dev * block_rows), jnp.float32),
        in_specs=[smem, smem] + [vmem] * 7
        + [pl.BlockSpec((together, *rows.shape[1:]), lambda i: (i, 0, 0))],
        out_specs=pl.BlockSpec((n_out, 1, chunk), lambda i: (0, 0, i)),
        scratch_shapes=[
            pltpu.VMEM((PANEL, chunk), jnp.float32),
            pltpu.VMEM((PANEL, chunk), jnp.float32),
            pltpu.VMEM((2 * PANEL + n_own, FEAT), jnp.float32),
        ],
        compiler_params=pltpu.CompilerParams(vmem_limit_bytes=40 * 1024 * 1024),
    )(numbers, position, panel, trail, scales, one, two, second, table, rows)


def on_device(points, feature_scales, amplitude, ridge):
    n_row = lax.axis_size("row")
    n_col = lax.axis_size("col")
    block_rows = points.shape[0] // n_row
    numbers = jnp.concatenate([amplitude, ridge])
    position = jnp.stack([lax.axis_index("row"), lax.axis_index("col")]).astype(jnp.int32)
    scales = feature_scales[None]
    factored = exchange_and_factor(numbers, points, scales, n_row, n_col)
    finished = slab(numbers, position, factored, scales, n_row, n_col, block_rows)
    return finished.reshape(SLAB // (BLK * n_col), 1, BLK, 1, -1)


def solution(mesh):
    placed = (P(("row", "col"), None), P(), P(), P())
    return jax.shard_map(
        on_device,
        mesh=mesh,
        in_specs=placed,
        out_specs=P(None, "col", None, "row", None),
        check_vma=False,
    )
```

```python
import functools

import jax
import jax.numpy as jnp
from jax import lax
from jax.experimental import pallas as pl
from jax.experimental.pallas import tpu as pltpu
from jax.sharding import PartitionSpec as P

FEAT = 64
SLAB = 1536
PANEL = 256
BLK = 16
BASE = 64
SUB = 8
HIGHEST = lax.Precision.HIGHEST
MESH = pl.DeviceIdType.MESH


def pack(rows):
    half = rows.shape[-2] // 2
    return jnp.concatenate([rows[..., :half, :], rows[..., half:, :]], axis=-1)


def unpack(rows):
    return jnp.concatenate([rows[..., :FEAT], rows[..., FEAT:]], axis=-2)


def split(x):
    high = x.astype(jnp.bfloat16)
    rest = x - high.astype(jnp.float32)
    middle = rest.astype(jnp.bfloat16)
    low = (rest - middle.astype(jnp.float32)).astype(jnp.bfloat16)
    return high, middle, low


def joined_dot(a, b, dims):
    ah, am, al = split(a)
    bh, bm, bl = split(b)
    left = jnp.concatenate([ah, ah, am, ah, al, am], axis=dims[0][0])
    right = jnp.concatenate([bh, bm, bh, bl, bh, bm], axis=dims[1][0])
    return lax.dot_general(left, right, (dims, ((), ())), preferred_element_type=jnp.float32)


def gaussian(left, right, signal):
    left_norms = 0.5 * jnp.sum(left * left, axis=1, keepdims=True)
    right_norms = full_dot(jnp.full((8, FEAT), 0.5, jnp.float32), right * right, ((1,), (1,)))[:1]
    cross = joined_dot(left, right, ((1,), (1,)))
    return signal * jnp.exp(cross - left_norms - right_norms)


def factor_kernel(
    n_row, n_col, n_panel, n_trail,
    numbers, points, scales,
    rows_out, panel_out, trail_out, inverse_one, inverse_two, second_rows, own_table, scale_out,
    turned, blocks, strips, work_a, work_x,
    send_sem, recv_sem, trail_send, trail_recv, panel_send, panel_recv, local_sem,
):
    n_dev = n_row * n_col
    my_row = lax.axis_index("row")
    my_col = lax.axis_index("col")
    me = my_row * n_col + my_col
    has_trail = jnp.logical_and(me >= n_panel, me < n_panel + n_trail)
    has_panel = me < n_panel

    def place(step):
        peer = lax.rem(me + step, n_dev)
        return peer, lax.div(peer, n_col), lax.rem(peer, n_col)

    barrier = pltpu.get_barrier_semaphore()

    @pl.loop(1, n_dev)
    def _(step):
        _, row, col = place(step)
        pl.semaphore_signal(barrier, inc=1, device_id=(row, col), device_id_type=MESH)

    fetches = [
        pltpu.make_async_copy(points, turned, local_sem.at[1]),
        pltpu.make_async_copy(scales, scale_out, local_sem.at[2]),
    ]
    for fetch in fetches:
        fetch.start()
    for fetch in fetches:
        fetch.wait()
    values = turned[...].T
    blocks[...] = pack(values.reshape(blocks.shape[0], -1, FEAT))
    strips[...] = pack(values.reshape(strips.shape[0], strips.shape[1], BLK, FEAT))
    pl.semaphore_wait(barrier, n_dev - 1)

    def block_copy(step):
        _, row, col = place(step)
        return pltpu.make_async_remote_copy(
            src_ref=blocks.at[row], dst_ref=rows_out.at[me],
            send_sem=send_sem.at[step], recv_sem=recv_sem.at[me],
            device_id=(row, col), device_id_type=MESH,
        )

    def trail_copy(step):
        _, row, col = place(step)
        return pltpu.make_async_remote_copy(
            src_ref=strips.at[:, col], dst_ref=trail_out.at[me - n_panel],
            send_sem=trail_send.at[step], recv_sem=trail_recv.at[me - n_panel],
            device_id=(row, col), device_id_type=MESH,
        )

    def panel_copy(source, step):
        row = lax.rem(my_row + step, n_row)
        return pltpu.make_async_remote_copy(
            src_ref=rows_out.at[source], dst_ref=panel_out.at[source, my_row],
            send_sem=panel_send.at[source, step], recv_sem=panel_recv.at[source, my_row],
            device_id=(row, my_col), device_id_type=MESH,
        )

    def arrival(source):
        return pltpu.make_async_remote_copy(
            src_ref=blocks.at[0], dst_ref=rows_out.at[source],
            send_sem=send_sem.at[0], recv_sem=recv_sem.at[source],
            device_id=(my_row, my_col), device_id_type=MESH,
        )

    def send_blocks():
        @pl.loop(1, n_dev)
        def _(step):
            block_copy(step).start()

    pl.when(has_panel)(send_blocks)

    own = pltpu.make_async_copy(blocks.at[my_row], rows_out.at[me], local_sem.at[0])
    own.start()
    own.wait()

    for source in range(n_panel):
        @pl.when(me != source)
        def _():
            arrival(source).wait_recv()

        kept = pltpu.make_async_copy(
            rows_out.at[source], panel_out.at[source, my_row], local_sem.at[0]
        )
        kept.start()
        for step in range(1, n_row):
            panel_copy(source, step).start()
        kept.wait()

    @pl.when(has_trail)
    def _():
        @pl.loop(1, n_dev)
        def _(step):
            trail_copy(step).start()

        kept = pltpu.make_async_copy(
            strips.at[:, my_col], trail_out.at[me - n_panel], local_sem.at[0]
        )
        kept.start()
        kept.wait()

    pl.when(jnp.logical_not(has_panel))(send_blocks)

    for source in range(n_panel):
        for step in range(1, n_row):
            row = lax.rem(my_row + step, n_row)
            pltpu.make_async_remote_copy(
                src_ref=rows_out.at[source], dst_ref=panel_out.at[source, row],
                send_sem=panel_send.at[source, 0], recv_sem=panel_recv.at[source, row],
                device_id=(my_row, my_col), device_id_type=MESH,
            ).wait_recv()
            panel_copy(source, step).wait_send()

    signal = numbers[0]
    jitter = numbers[1]
    scale = scale_out[...]
    panel = unpack(panel_out[...]).reshape(2 * PANEL, FEAT) * scale
    center = gaussian(panel, panel, signal)
    row = lax.broadcasted_iota(jnp.int32, center.shape, 0)
    col = lax.broadcasted_iota(jnp.int32, center.shape, 1)
    center = center + jnp.where(row == col, jitter, 0.0)
    inverse_factor(center[:PANEL, :PANEL], inverse_one, work_a, work_x)
    low_first = full_dot(center[PANEL:, :PANEL], inverse_one[...], ((1,), (1,))).astype(jnp.bfloat16)
    second_rows[...] = low_first
    low_second = center[PANEL:, PANEL:] - plain_dot(low_first, low_first, ((1,), (1,)))
    inverse_factor(low_second, inverse_two, work_a, work_x)

    @pl.loop(0, n_trail)
    def _(source):
        @pl.when(me != source + n_panel)
        def _():
            pltpu.make_async_remote_copy(
                src_ref=strips.at[:, my_col], dst_ref=trail_out.at[source],
                send_sem=trail_send.at[0], recv_sem=trail_recv.at[source],
                device_id=(my_row, my_col), device_id_type=MESH,
            ).wait_recv()

    owned = unpack(trail_out[...]).reshape(-1, FEAT) * scale
    own = gaussian(owned, panel, signal)
    own_first = full_dot(own[:, :PANEL], inverse_one[...], ((1,), (1,))).astype(jnp.bfloat16)
    own_second = own[:, PANEL:] - plain_dot(own_first, low_first, ((1,), (1,)))
    own_table[:, :PANEL] = own_first
    own_table[:, PANEL:] = full_dot(own_second, inverse_two[...], ((1,), (1,))).astype(jnp.bfloat16)

    @pl.loop(n_panel, n_dev)
    def _(source):
        @pl.when(me != source)
        def _():
            arrival(source).wait_recv()

    @pl.loop(1, n_dev)
    def _(step):
        block_copy(step).wait_send()

    @pl.when(has_trail)
    def _():
        @pl.loop(1, n_dev)
        def _(step):
            trail_copy(step).wait_send()


def exchange_and_factor(numbers, points, scales, n_row, n_col):
    rows_one = points.shape[0]
    n_dev = n_row * n_col
    n_panel = 2 * PANEL // rows_one
    n_trail = SLAB // rows_one - n_panel
    strips_one = rows_one // (BLK * n_col)
    piece = (rows_one // n_row // 2, 2 * FEAT)
    strip = (BLK // 2, 2 * FEAT)
    n_own = n_trail * strips_one * BLK
    vmem = pl.BlockSpec(memory_space=pltpu.VMEM)
    whole = pl.BlockSpec(memory_space=pl.ANY)
    shape = jax.ShapeDtypeStruct
    return pl.pallas_call(
        functools.partial(factor_kernel, n_row, n_col, n_panel, n_trail),
        out_shape=(
            shape((n_dev, *piece), jnp.float32),
            shape((n_panel, n_row, *piece), jnp.float32),
            shape((n_trail, strips_one, *strip), jnp.float32),
            shape((PANEL, PANEL), jnp.float32),
            shape((PANEL, PANEL), jnp.float32),
            shape((PANEL, PANEL), jnp.bfloat16),
            shape((n_own, 2 * PANEL), jnp.bfloat16),
            shape((1, FEAT), jnp.float32),
        ),
        in_specs=[pl.BlockSpec(memory_space=pltpu.SMEM), whole, whole],
        out_specs=(vmem,) * 8,
        scratch_shapes=[
            pltpu.VMEM((FEAT, rows_one), jnp.float32),
            pltpu.VMEM((n_row, *piece), jnp.float32),
            pltpu.VMEM((strips_one, n_col, *strip), jnp.float32),
            pltpu.VMEM((PANEL, PANEL), jnp.float32),
            pltpu.VMEM((PANEL, PANEL), jnp.float32),
            pltpu.SemaphoreType.DMA((n_dev,)),
            pltpu.SemaphoreType.DMA((n_dev,)),
            pltpu.SemaphoreType.DMA((n_dev,)),
            pltpu.SemaphoreType.DMA((n_trail,)),
            pltpu.SemaphoreType.DMA((n_panel, n_row)),
            pltpu.SemaphoreType.DMA((n_panel, n_row)),
            pltpu.SemaphoreType.DMA((3,)),
        ],
        compiler_params=pltpu.CompilerParams(
            collective_id=0, has_side_effects=True, vmem_limit_bytes=40 * 1024 * 1024
        ),
    )(numbers, points.T, scales)


def base_inverse(block):
    row = lax.broadcasted_iota(jnp.int32, (BASE, BASE), 0)
    col = lax.broadcasted_iota(jnp.int32, (BASE, BASE), 1)
    both = jnp.concatenate([block, (row == col).astype(jnp.float32)], axis=1)
    groups = BASE // SUB
    done = []
    for g in range(groups):
        height = BASE - SUB * g
        shape = (height, 2 * BASE)
        inside = lax.broadcasted_iota(jnp.int32, shape, 0)
        cols = [jnp.broadcast_to(both[:, SUB * g + j : SUB * g + j + 1], shape) for j in range(SUB)]
        pairs = []
        for j in range(0, SUB, 2):
            one, two = cols[j], cols[j + 1]
            a, b, d = one[j : j + 1], one[j + 1 : j + 2], two[j + 1 : j + 2]
            pairs.append((a, b, d))
            inverse = pl.reciprocal(a * d - b * b)
            first = jnp.where(inside > j + 1, one, 0.0)
            second = jnp.where(inside > j + 1, two, 0.0)

            def solved(u, v):
                return (d * u - b * v) * inverse, (a * v - b * u) * inverse

            for k in range(j + 2, SUB):
                u, v = solved(one[k : k + 1], two[k : k + 1])
                cols[k] = cols[k] - (first * u + second * v)
            u, v = solved(both[j : j + 1], both[j + 1 : j + 2])
            both = both - (first * u + second * v)
        top = both[:SUB, BASE:]
        lines = []
        for j, (a, b, d) in zip(range(0, SUB, 2), pairs):
            a, b, d = a[:, :BASE], b[:, :BASE], d[:, :BASE]
            ratio = b / a
            lines.append(top[j : j + 1] * lax.rsqrt(a))
            lines.append((top[j + 1 : j + 2] - ratio * top[j : j + 1]) * lax.rsqrt(d - b * ratio))
        done.append(jnp.concatenate(lines, axis=0))
        both = both[SUB:]
    return jnp.concatenate(done, axis=0)


def full_dot(a, b, dims=((1,), (0,))):
    return lax.dot_general(
        a, b, (dims, ((), ())), precision=HIGHEST, preferred_element_type=jnp.float32
    )


def plain_dot(a, b, dims=((1,), (0,))):
    return lax.dot_general(a, b, (dims, ((), ())), preferred_element_type=jnp.float32)


def inverse_factor(a, out_ref, work_a, work_x):
    work_a[...] = (a + a.T) * 0.5
    row = lax.broadcasted_iota(jnp.int32, (PANEL, PANEL), 0)
    col = lax.broadcasted_iota(jnp.int32, (PANEL, PANEL), 1)
    work_x[...] = (row == col).astype(jnp.float32)
    out_ref[...] = jnp.zeros((PANEL, PANEL), jnp.float32)
    for start in range(0, PANEL, BASE):
        stop = start + BASE
        first = start // 128 * 128
        last = (stop + 127) // 128 * 128
        inverse = base_inverse(work_a[start:stop, start:stop])
        solved_x = joined_dot(inverse, work_x[start:stop, :last], ((1,), (0,)))
        out_ref[start:stop, :last] = solved_x
        if stop == PANEL:
            break
        solved_a = joined_dot(inverse, work_a[start:stop, first:], ((1,), (0,)))
        below = solved_a[:, stop - first :]
        kept = stop // 128 * 128
        work_a[stop:, kept:] -= joined_dot(below, solved_a[:, kept - first :], ((0,), (0,)))
        work_x[stop:, :last] -= joined_dot(below, solved_x, ((0,), (0,)))


def slab_kernel(
    n_row, n_col, block_rows,
    numbers, position, panel_ref, trail_ref, scales, one_ref, two_ref, second_ref, table_ref, rows_ref,
    out_ref, keep_one, keep_two, chosen_ref,
):
    signal = numbers[0]
    jitter = numbers[1]
    process_row = position[0]
    column = position[1]
    scale = scales[...]

    @pl.when(pl.program_id(0) == 0)
    def _():
        chosen_ref[: 2 * PANEL] = unpack(panel_ref[...]).reshape(2 * PANEL, FEAT) * scale
        chosen_ref[2 * PANEL :] = unpack(trail_ref[...]).reshape(-1, FEAT) * scale

    chunk = rows_ref.shape[0] * block_rows
    points = unpack(rows_ref[...]).reshape(chunk, FEAT) * scale
    kernel = gaussian(chosen_ref[...], points, signal)
    shape = kernel.shape
    group = BLK * n_col
    col = lax.broadcasted_iota(jnp.int32, (shape[0], 1), 0)
    extra = col - 2 * PANEL
    owned = 2 * PANEL + extra // BLK * group + column * BLK + extra % BLK
    col = jnp.where(extra >= 0, owned, col)
    place = pl.program_id(0) * chunk + lax.broadcasted_iota(jnp.int32, (1, chunk), 1)
    row = (place // block_rows * n_row + process_row) * block_rows + place % block_rows
    kernel = kernel + jnp.where(col == row, jitter, 0.0)
    first = full_dot(one_ref[...], kernel[:PANEL]).astype(jnp.bfloat16)
    reduced = kernel[PANEL : 2 * PANEL] - plain_dot(second_ref[...], first)
    second = full_dot(two_ref[...], reduced).astype(jnp.bfloat16)
    trailing = kernel[2 * PANEL :] - (
        plain_dot(table_ref[:, :PANEL], first) + plain_dot(table_ref[:, PANEL:], second)
    )
    keep_one[...] = first.astype(jnp.float32)
    keep_two[...] = second.astype(jnp.float32)
    blocks = PANEL // group
    for which, keep in enumerate((keep_one, keep_two)):
        for t in range(blocks):
            start = pl.multiple_of(t * group + column * BLK, BLK)
            at = (which * blocks + t) * BLK
            out_ref[at : at + BLK] = keep[pl.ds(start, BLK), :].reshape(BLK, 1, chunk)
    out_ref[2 * blocks * BLK :] = trailing.reshape(trailing.shape[0], 1, chunk)


def slab(numbers, position, factored, n_row, n_col, block_rows):
    rows, panel, trail, one, two, second, table, scales = factored
    n_dev = n_row * n_col
    together = 512 // block_rows
    chunk = together * block_rows
    n_own = table.shape[0]
    n_out = n_own + 2 * PANEL // n_col
    vmem = pl.BlockSpec(memory_space=pltpu.VMEM)
    smem = pl.BlockSpec(memory_space=pltpu.SMEM)
    return pl.pallas_call(
        functools.partial(slab_kernel, n_row, n_col, block_rows),
        grid=(n_dev // together,),
        out_shape=jax.ShapeDtypeStruct((n_out, 1, n_dev * block_rows), jnp.float32),
        in_specs=[smem, smem] + [vmem] * 7
        + [pl.BlockSpec((together, *rows.shape[1:]), lambda i: (i, 0, 0))],
        out_specs=pl.BlockSpec((n_out, 1, chunk), lambda i: (0, 0, i)),
        scratch_shapes=[
            pltpu.VMEM((PANEL, chunk), jnp.float32),
            pltpu.VMEM((PANEL, chunk), jnp.float32),
            pltpu.VMEM((2 * PANEL + n_own, FEAT), jnp.float32),
        ],
        compiler_params=pltpu.CompilerParams(vmem_limit_bytes=40 * 1024 * 1024),
    )(numbers, position, panel, trail, scales, one, two, second, table, rows)


def on_device(points, feature_scales, amplitude, ridge):
    n_row = lax.axis_size("row")
    n_col = lax.axis_size("col")
    block_rows = points.shape[0] // n_row
    numbers = jnp.concatenate([amplitude, ridge])
    position = jnp.stack([lax.axis_index("row"), lax.axis_index("col")]).astype(jnp.int32)
    scales = feature_scales[None]
    factored = exchange_and_factor(numbers, points, scales, n_row, n_col)
    finished = slab(numbers, position, factored, n_row, n_col, block_rows)
    return finished.reshape(SLAB // (BLK * n_col), 1, BLK, 1, -1)


def solution(mesh):
    placed = (P(("row", "col"), None), P(), P(), P())
    return jax.shard_map(
        on_device,
        mesh=mesh,
        in_specs=placed,
        out_specs=P(None, "col", None, "row", None),
        check_vma=False,
    )
```

```python
import functools

import jax
import jax.numpy as jnp
from jax import lax
from jax.experimental import pallas as pl
from jax.experimental.pallas import tpu as pltpu
from jax.sharding import PartitionSpec as P

FEAT = 64
SLAB = 1536
PANEL = 256
BLK = 16
BASE = 64
SUB = 8
HIGHEST = lax.Precision.HIGHEST
MESH = pl.DeviceIdType.MESH


def pack(rows):
    half = rows.shape[-2] // 2
    return jnp.concatenate([rows[..., :half, :], rows[..., half:, :]], axis=-1)


def unpack(rows):
    return jnp.concatenate([rows[..., :FEAT], rows[..., FEAT:]], axis=-2)


def split(x):
    high = x.astype(jnp.bfloat16)
    rest = x - high.astype(jnp.float32)
    middle = rest.astype(jnp.bfloat16)
    low = (rest - middle.astype(jnp.float32)).astype(jnp.bfloat16)
    return high, middle, low


def joined_dot(a, b, dims):
    ah, am, al = split(a)
    bh, bm, bl = split(b)
    left = jnp.concatenate([ah, ah, am, ah, al, am], axis=dims[0][0])
    right = jnp.concatenate([bh, bm, bh, bl, bh, bm], axis=dims[1][0])
    return lax.dot_general(left, right, (dims, ((), ())), preferred_element_type=jnp.float32)


def gaussian(left, right, signal):
    left_norms = 0.5 * jnp.sum(left * left, axis=1, keepdims=True)
    right_norms = full_dot(jnp.full((8, FEAT), 0.5, jnp.float32), right * right, ((1,), (1,)))[:1]
    cross = joined_dot(left, right, ((1,), (1,)))
    return signal * jnp.exp(cross - left_norms - right_norms)


def factor_kernel(
    n_row, n_col, n_panel, n_trail,
    numbers, points, scales,
    rows_out, panel_out, trail_out, inverse_one, inverse_two, second_rows, own_table,
    blocks, strips, work_a, work_x,
    send_sem, recv_sem, trail_send, trail_recv, panel_send, panel_recv, local_sem,
):
    n_dev = n_row * n_col
    my_row = lax.axis_index("row")
    my_col = lax.axis_index("col")
    me = my_row * n_col + my_col
    has_trail = jnp.logical_and(me >= n_panel, me < n_panel + n_trail)
    has_panel = me < n_panel
    values = points[...]
    blocks[...] = pack(values.reshape(blocks.shape[0], -1, FEAT))
    strips[...] = pack(values.reshape(strips.shape[0], strips.shape[1], BLK, FEAT))

    def place(step):
        peer = lax.rem(me + step, n_dev)
        return peer, lax.div(peer, n_col), lax.rem(peer, n_col)

    barrier = pltpu.get_barrier_semaphore()

    @pl.loop(1, n_dev)
    def _(step):
        _, row, col = place(step)
        pl.semaphore_signal(barrier, inc=1, device_id=(row, col), device_id_type=MESH)

    pl.semaphore_wait(barrier, n_dev - 1)

    def block_copy(step):
        _, row, col = place(step)
        return pltpu.make_async_remote_copy(
            src_ref=blocks.at[row], dst_ref=rows_out.at[me],
            send_sem=send_sem.at[step], recv_sem=recv_sem.at[me],
            device_id=(row, col), device_id_type=MESH,
        )

    def trail_copy(step):
        _, row, col = place(step)
        return pltpu.make_async_remote_copy(
            src_ref=strips.at[:, col], dst_ref=trail_out.at[me - n_panel],
            send_sem=trail_send.at[step], recv_sem=trail_recv.at[me - n_panel],
            device_id=(row, col), device_id_type=MESH,
        )

    def panel_copy(source, step):
        row = lax.rem(my_row + step, n_row)
        return pltpu.make_async_remote_copy(
            src_ref=rows_out.at[source], dst_ref=panel_out.at[source, my_row],
            send_sem=panel_send.at[source, step], recv_sem=panel_recv.at[source, my_row],
            device_id=(row, my_col), device_id_type=MESH,
        )

    def arrival(source):
        return pltpu.make_async_remote_copy(
            src_ref=blocks.at[0], dst_ref=rows_out.at[source],
            send_sem=send_sem.at[0], recv_sem=recv_sem.at[source],
            device_id=(my_row, my_col), device_id_type=MESH,
        )

    def send_blocks():
        @pl.loop(1, n_dev)
        def _(step):
            block_copy(step).start()

    pl.when(has_panel)(send_blocks)

    own = pltpu.make_async_copy(blocks.at[my_row], rows_out.at[me], local_sem.at[0])
    own.start()
    own.wait()

    for source in range(n_panel):
        @pl.when(me != source)
        def _():
            arrival(source).wait_recv()

        kept = pltpu.make_async_copy(
            rows_out.at[source], panel_out.at[source, my_row], local_sem.at[0]
        )
        kept.start()
        for step in range(1, n_row):
            panel_copy(source, step).start()
        kept.wait()

    @pl.when(has_trail)
    def _():
        @pl.loop(1, n_dev)
        def _(step):
            trail_copy(step).start()

        kept = pltpu.make_async_copy(
            strips.at[:, my_col], trail_out.at[me - n_panel], local_sem.at[0]
        )
        kept.start()
        kept.wait()

    pl.when(jnp.logical_not(has_panel))(send_blocks)

    for source in range(n_panel):
        for step in range(1, n_row):
            row = lax.rem(my_row + step, n_row)
            pltpu.make_async_remote_copy(
                src_ref=rows_out.at[source], dst_ref=panel_out.at[source, row],
                send_sem=panel_send.at[source, 0], recv_sem=panel_recv.at[source, row],
                device_id=(my_row, my_col), device_id_type=MESH,
            ).wait_recv()
            panel_copy(source, step).wait_send()

    signal = numbers[0]
    jitter = numbers[1]
    scale = scales[...]
    panel = unpack(panel_out[...]).reshape(2 * PANEL, FEAT) * scale
    center = gaussian(panel, panel, signal)
    row = lax.broadcasted_iota(jnp.int32, center.shape, 0)
    col = lax.broadcasted_iota(jnp.int32, center.shape, 1)
    center = center + jnp.where(row == col, jitter, 0.0)
    inverse_factor(center[:PANEL, :PANEL], inverse_one, work_a, work_x)
    @pl.loop(0, n_trail)
    def _(source):
        @pl.when(me != source + n_panel)
        def _():
            pltpu.make_async_remote_copy(
                src_ref=strips.at[:, my_col], dst_ref=trail_out.at[source],
                send_sem=trail_send.at[0], recv_sem=trail_recv.at[source],
                device_id=(my_row, my_col), device_id_type=MESH,
            ).wait_recv()

    low_first = full_dot(center[PANEL:, :PANEL], inverse_one[...], ((1,), (1,))).astype(jnp.bfloat16)
    second_rows[...] = low_first
    low_second = center[PANEL:, PANEL:] - plain_dot(low_first, low_first, ((1,), (1,)))
    owned = unpack(trail_out[...]).reshape(-1, FEAT) * scale
    own = gaussian(owned, panel, signal)
    own_first = full_dot(own[:, :PANEL], inverse_one[...], ((1,), (1,))).astype(jnp.bfloat16)
    own_second = own[:, PANEL:] - plain_dot(own_first, low_first, ((1,), (1,)))
    own_table[:, :PANEL] = own_first
    inverse_factor(low_second, inverse_two, work_a, work_x)
    own_table[:, PANEL:] = full_dot(own_second, inverse_two[...], ((1,), (1,))).astype(jnp.bfloat16)

    @pl.loop(n_panel, n_dev)
    def _(source):
        @pl.when(me != source)
        def _():
            arrival(source).wait_recv()

    @pl.loop(1, n_dev)
    def _(step):
        block_copy(step).wait_send()

    @pl.when(has_trail)
    def _():
        @pl.loop(1, n_dev)
        def _(step):
            trail_copy(step).wait_send()


def exchange_and_factor(numbers, points, scales, n_row, n_col):
    rows_one = points.shape[0]
    n_dev = n_row * n_col
    n_panel = 2 * PANEL // rows_one
    n_trail = SLAB // rows_one - n_panel
    strips_one = rows_one // (BLK * n_col)
    piece = (rows_one // n_row // 2, 2 * FEAT)
    strip = (BLK // 2, 2 * FEAT)
    n_own = n_trail * strips_one * BLK
    vmem = pl.BlockSpec(memory_space=pltpu.VMEM)
    shape = jax.ShapeDtypeStruct
    return pl.pallas_call(
        functools.partial(factor_kernel, n_row, n_col, n_panel, n_trail),
        out_shape=(
            shape((n_dev, *piece), jnp.float32),
            shape((n_panel, n_row, *piece), jnp.float32),
            shape((n_trail, strips_one, *strip), jnp.float32),
            shape((PANEL, PANEL), jnp.float32),
            shape((PANEL, PANEL), jnp.float32),
            shape((PANEL, PANEL), jnp.bfloat16),
            shape((n_own, 2 * PANEL), jnp.bfloat16),
        ),
        in_specs=[pl.BlockSpec(memory_space=pltpu.SMEM), vmem, vmem],
        out_specs=(vmem,) * 7,
        scratch_shapes=[
            pltpu.VMEM((n_row, *piece), jnp.float32),
            pltpu.VMEM((strips_one, n_col, *strip), jnp.float32),
            pltpu.VMEM((PANEL, PANEL), jnp.float32),
            pltpu.VMEM((PANEL, PANEL), jnp.float32),
            pltpu.SemaphoreType.DMA((n_dev,)),
            pltpu.SemaphoreType.DMA((n_dev,)),
            pltpu.SemaphoreType.DMA((n_dev,)),
            pltpu.SemaphoreType.DMA((n_trail,)),
            pltpu.SemaphoreType.DMA((n_panel, n_row)),
            pltpu.SemaphoreType.DMA((n_panel, n_row)),
            pltpu.SemaphoreType.DMA((1,)),
        ],
        compiler_params=pltpu.CompilerParams(
            collective_id=0, has_side_effects=True, vmem_limit_bytes=40 * 1024 * 1024
        ),
    )(numbers, points, scales)


def base_inverse(block):
    row = lax.broadcasted_iota(jnp.int32, (BASE, BASE), 0)
    col = lax.broadcasted_iota(jnp.int32, (BASE, BASE), 1)
    both = jnp.concatenate([block, (row == col).astype(jnp.float32)], axis=1)
    groups = BASE // SUB
    done = []
    for g in range(groups):
        height = BASE - SUB * g
        shape = (height, 2 * BASE)
        inside = lax.broadcasted_iota(jnp.int32, shape, 0)
        cols = [jnp.broadcast_to(both[:, SUB * g + j : SUB * g + j + 1], shape) for j in range(SUB)]
        scale = jnp.zeros((SUB, BASE), jnp.float32)
        for j in range(SUB):
            pivot = cols[j][j : j + 1]
            inverse = 1.0 / pivot
            scale = jnp.where(inside[:SUB, :BASE] == j, lax.rsqrt(pivot[:, :BASE]), scale)
            factors = jnp.where(inside > j, cols[j], 0.0)
            for k in range(j + 1, SUB):
                cols[k] = cols[k] - factors * (cols[j][k : k + 1] * inverse)
            both = both - factors * (both[j : j + 1] * inverse)
        done.append(both[:SUB, BASE:] * scale)
        both = both[SUB:]
    return jnp.concatenate(done, axis=0)


def full_dot(a, b, dims=((1,), (0,))):
    return lax.dot_general(
        a, b, (dims, ((), ())), precision=HIGHEST, preferred_element_type=jnp.float32
    )


def plain_dot(a, b, dims=((1,), (0,))):
    return lax.dot_general(a, b, (dims, ((), ())), preferred_element_type=jnp.float32)


def inverse_factor(a, out_ref, work_a, work_x):
    work_a[...] = (a + a.T) * 0.5
    row = lax.broadcasted_iota(jnp.int32, (PANEL, PANEL), 0)
    col = lax.broadcasted_iota(jnp.int32, (PANEL, PANEL), 1)
    work_x[...] = (row == col).astype(jnp.float32)
    out_ref[...] = jnp.zeros((PANEL, PANEL), jnp.float32)
    for start in range(0, PANEL, BASE):
        stop = start + BASE
        first = start // 128 * 128
        last = (stop + 127) // 128 * 128
        inverse = base_inverse(work_a[start:stop, start:stop])
        solved_x = joined_dot(inverse, work_x[start:stop, :last], ((1,), (0,)))
        out_ref[start:stop, :last] = solved_x
        if stop == PANEL:
            break
        solved_a = joined_dot(inverse, work_a[start:stop, first:], ((1,), (0,)))
        below = joined_dot(work_a[stop:, start:stop], inverse, ((1,), (1,)))
        kept = stop // 128 * 128
        work_a[stop:, kept:] -= joined_dot(below, solved_a[:, kept - first :], ((1,), (0,)))
        work_x[stop:, :last] -= joined_dot(below, solved_x, ((1,), (0,)))


def slab_kernel(
    n_row, n_col, block_rows,
    numbers, position, panel_ref, trail_ref, scales, one_ref, two_ref, second_ref, table_ref, rows_ref,
    out_ref, keep_one, keep_two, chosen_ref,
):
    signal = numbers[0]
    jitter = numbers[1]
    process_row = position[0]
    column = position[1]
    scale = scales[...]

    @pl.when(pl.program_id(0) == 0)
    def _():
        chosen_ref[: 2 * PANEL] = unpack(panel_ref[...]).reshape(2 * PANEL, FEAT) * scale
        chosen_ref[2 * PANEL :] = unpack(trail_ref[...]).reshape(-1, FEAT) * scale

    chunk = rows_ref.shape[0] * block_rows
    points = unpack(rows_ref[...]).reshape(chunk, FEAT) * scale
    kernel = gaussian(chosen_ref[...], points, signal)
    shape = kernel.shape
    group = BLK * n_col
    col = lax.broadcasted_iota(jnp.int32, (shape[0], 1), 0)
    extra = col - 2 * PANEL
    owned = 2 * PANEL + extra // BLK * group + column * BLK + extra % BLK
    col = jnp.where(extra >= 0, owned, col)
    place = pl.program_id(0) * chunk + lax.broadcasted_iota(jnp.int32, (1, chunk), 1)
    row = (place // block_rows * n_row + process_row) * block_rows + place % block_rows
    kernel = kernel + jnp.where(col == row, jitter, 0.0)
    first = full_dot(one_ref[...], kernel[:PANEL]).astype(jnp.bfloat16)
    reduced = kernel[PANEL : 2 * PANEL] - plain_dot(second_ref[...], first)
    second = full_dot(two_ref[...], reduced).astype(jnp.bfloat16)
    trailing = kernel[2 * PANEL :] - (
        plain_dot(table_ref[:, :PANEL], first) + plain_dot(table_ref[:, PANEL:], second)
    )
    keep_one[...] = first.astype(jnp.float32)
    keep_two[...] = second.astype(jnp.float32)
    blocks = PANEL // group
    for which, keep in enumerate((keep_one, keep_two)):
        for t in range(blocks):
            start = pl.multiple_of(t * group + column * BLK, BLK)
            at = (which * blocks + t) * BLK
            out_ref[at : at + BLK] = keep[pl.ds(start, BLK), :].reshape(BLK, 1, chunk)
    out_ref[2 * blocks * BLK :] = trailing.reshape(trailing.shape[0], 1, chunk)


def slab(numbers, position, factored, scales, n_row, n_col, block_rows):
    rows, panel, trail, one, two, second, table = factored
    n_dev = n_row * n_col
    together = 512 // block_rows
    chunk = together * block_rows
    n_own = table.shape[0]
    n_out = n_own + 2 * PANEL // n_col
    vmem = pl.BlockSpec(memory_space=pltpu.VMEM)
    smem = pl.BlockSpec(memory_space=pltpu.SMEM)
    return pl.pallas_call(
        functools.partial(slab_kernel, n_row, n_col, block_rows),
        grid=(n_dev // together,),
        out_shape=jax.ShapeDtypeStruct((n_out, 1, n_dev * block_rows), jnp.float32),
        in_specs=[smem, smem] + [vmem] * 7
        + [pl.BlockSpec((together, *rows.shape[1:]), lambda i: (i, 0, 0))],
        out_specs=pl.BlockSpec((n_out, 1, chunk), lambda i: (0, 0, i)),
        scratch_shapes=[
            pltpu.VMEM((PANEL, chunk), jnp.float32),
            pltpu.VMEM((PANEL, chunk), jnp.float32),
            pltpu.VMEM((2 * PANEL + n_own, FEAT), jnp.float32),
        ],
        compiler_params=pltpu.CompilerParams(vmem_limit_bytes=40 * 1024 * 1024),
    )(numbers, position, panel, trail, scales, one, two, second, table, rows)


def on_device(points, feature_scales, amplitude, ridge):
    n_row = lax.axis_size("row")
    n_col = lax.axis_size("col")
    block_rows = points.shape[0] // n_row
    numbers = jnp.concatenate([amplitude, ridge])
    position = jnp.stack([lax.axis_index("row"), lax.axis_index("col")]).astype(jnp.int32)
    scales = feature_scales[None]
    factored = exchange_and_factor(numbers, points, scales, n_row, n_col)
    finished = slab(numbers, position, factored, scales, n_row, n_col, block_rows)
    return finished.reshape(SLAB // (BLK * n_col), 1, BLK, 1, -1)


def solution(mesh):
    placed = (P(("row", "col"), None), P(), P(), P())
    return jax.shard_map(
        on_device,
        mesh=mesh,
        in_specs=placed,
        out_specs=P(None, "col", None, "row", None),
        check_vma=False,
    )
```

```python
import functools

import jax
import jax.numpy as jnp
from jax import lax
from jax.experimental import pallas as pl
from jax.experimental.pallas import tpu as pltpu
from jax.sharding import PartitionSpec as P

FEAT = 64
SLAB = 1536
PANEL = 256
BLK = 16
BASE = 64
SUB = 8
HIGHEST = lax.Precision.HIGHEST
MESH = pl.DeviceIdType.MESH


def pack(rows):
    half = rows.shape[-2] // 2
    return jnp.concatenate([rows[..., :half, :], rows[..., half:, :]], axis=-1)


def unpack(rows):
    return jnp.concatenate([rows[..., :FEAT], rows[..., FEAT:]], axis=-2)


def split(x):
    high = x.astype(jnp.bfloat16)
    rest = x - high.astype(jnp.float32)
    middle = rest.astype(jnp.bfloat16)
    low = (rest - middle.astype(jnp.float32)).astype(jnp.bfloat16)
    return high, middle, low


def joined_dot(a, b, dims):
    ah, am, al = split(a)
    bh, bm, bl = split(b)
    left = jnp.concatenate([ah, ah, am, ah, al, am], axis=dims[0][0])
    right = jnp.concatenate([bh, bm, bh, bl, bh, bm], axis=dims[1][0])
    return lax.dot_general(left, right, (dims, ((), ())), preferred_element_type=jnp.float32)


def gaussian(left, right, signal):
    left_norms = 0.5 * jnp.sum(left * left, axis=1, keepdims=True)
    right_norms = full_dot(jnp.full((8, FEAT), 0.5, jnp.float32), right * right, ((1,), (1,)))[:1]
    cross = joined_dot(left, right, ((1,), (1,)))
    return signal * jnp.exp(cross - left_norms - right_norms)


def factor_kernel(
    n_row, n_col, n_panel, n_trail,
    numbers, points, scales,
    rows_out, panel_out, trail_out, inverse_one, inverse_two, second_rows, own_table,
    blocks, strips, work_a, work_x,
    send_sem, recv_sem, trail_send, trail_recv, panel_send, panel_recv, local_sem,
):
    n_dev = n_row * n_col
    my_row = lax.axis_index("row")
    my_col = lax.axis_index("col")
    me = my_row * n_col + my_col
    has_trail = jnp.logical_and(me >= n_panel, me < n_panel + n_trail)
    has_panel = me < n_panel
    values = points[...]
    blocks[...] = pack(values.reshape(blocks.shape[0], -1, FEAT))
    strips[...] = pack(values.reshape(strips.shape[0], strips.shape[1], BLK, FEAT))

    def place(step):
        peer = lax.rem(me + step, n_dev)
        return peer, lax.div(peer, n_col), lax.rem(peer, n_col)

    barrier = pltpu.get_barrier_semaphore()

    @pl.loop(1, n_dev)
    def _(step):
        _, row, col = place(step)
        pl.semaphore_signal(barrier, inc=1, device_id=(row, col), device_id_type=MESH)

    pl.semaphore_wait(barrier, n_dev - 1)

    def block_copy(step):
        _, row, col = place(step)
        return pltpu.make_async_remote_copy(
            src_ref=blocks.at[row], dst_ref=rows_out.at[me],
            send_sem=send_sem.at[step], recv_sem=recv_sem.at[me],
            device_id=(row, col), device_id_type=MESH,
        )

    def trail_copy(step):
        _, row, col = place(step)
        return pltpu.make_async_remote_copy(
            src_ref=strips.at[:, col], dst_ref=trail_out.at[me - n_panel],
            send_sem=trail_send.at[step], recv_sem=trail_recv.at[me - n_panel],
            device_id=(row, col), device_id_type=MESH,
        )

    def panel_copy(source, step):
        row = lax.rem(my_row + step, n_row)
        return pltpu.make_async_remote_copy(
            src_ref=rows_out.at[source], dst_ref=panel_out.at[source, my_row],
            send_sem=panel_send.at[source, step], recv_sem=panel_recv.at[source, my_row],
            device_id=(row, my_col), device_id_type=MESH,
        )

    def arrival(source):
        return pltpu.make_async_remote_copy(
            src_ref=blocks.at[0], dst_ref=rows_out.at[source],
            send_sem=send_sem.at[0], recv_sem=recv_sem.at[source],
            device_id=(my_row, my_col), device_id_type=MESH,
        )

    def send_blocks():
        @pl.loop(1, n_dev)
        def _(step):
            block_copy(step).start()

    pl.when(has_panel)(send_blocks)

    own = pltpu.make_async_copy(blocks.at[my_row], rows_out.at[me], local_sem.at[0])
    own.start()
    own.wait()

    for source in range(n_panel):
        @pl.when(me != source)
        def _():
            arrival(source).wait_recv()

        kept = pltpu.make_async_copy(
            rows_out.at[source], panel_out.at[source, my_row], local_sem.at[0]
        )
        kept.start()
        for step in range(1, n_row):
            panel_copy(source, step).start()
        kept.wait()

    @pl.when(has_trail)
    def _():
        @pl.loop(1, n_dev)
        def _(step):
            trail_copy(step).start()

        kept = pltpu.make_async_copy(
            strips.at[:, my_col], trail_out.at[me - n_panel], local_sem.at[0]
        )
        kept.start()
        kept.wait()

    pl.when(jnp.logical_not(has_panel))(send_blocks)

    for source in range(n_panel):
        for step in range(1, n_row):
            row = lax.rem(my_row + step, n_row)
            pltpu.make_async_remote_copy(
                src_ref=rows_out.at[source], dst_ref=panel_out.at[source, row],
                send_sem=panel_send.at[source, 0], recv_sem=panel_recv.at[source, row],
                device_id=(my_row, my_col), device_id_type=MESH,
            ).wait_recv()
            panel_copy(source, step).wait_send()

    signal = numbers[0]
    jitter = numbers[1]
    scale = scales[...]
    panel = unpack(panel_out[...]).reshape(2 * PANEL, FEAT) * scale
    center = gaussian(panel, panel, signal)
    row = lax.broadcasted_iota(jnp.int32, center.shape, 0)
    col = lax.broadcasted_iota(jnp.int32, center.shape, 1)
    center = center + jnp.where(row == col, jitter, 0.0)
    inverse_factor(center[:PANEL, :PANEL], inverse_one, work_a, work_x)
    @pl.loop(0, n_trail)
    def _(source):
        @pl.when(me != source + n_panel)
        def _():
            pltpu.make_async_remote_copy(
                src_ref=strips.at[:, my_col], dst_ref=trail_out.at[source],
                send_sem=trail_send.at[0], recv_sem=trail_recv.at[source],
                device_id=(my_row, my_col), device_id_type=MESH,
            ).wait_recv()

    low_first = full_dot(center[PANEL:, :PANEL], inverse_one[...], ((1,), (1,))).astype(jnp.bfloat16)
    second_rows[...] = low_first
    low_second = center[PANEL:, PANEL:] - plain_dot(low_first, low_first, ((1,), (1,)))
    owned = unpack(trail_out[...]).reshape(-1, FEAT) * scale
    own = gaussian(owned, panel, signal)
    own_first = full_dot(own[:, :PANEL], inverse_one[...], ((1,), (1,))).astype(jnp.bfloat16)
    own_second = own[:, PANEL:] - plain_dot(own_first, low_first, ((1,), (1,)))
    own_table[:, :PANEL] = own_first
    inverse_factor(low_second, inverse_two, work_a, work_x)
    own_table[:, PANEL:] = full_dot(own_second, inverse_two[...], ((1,), (1,))).astype(jnp.bfloat16)

    @pl.loop(n_panel, n_dev)
    def _(source):
        @pl.when(me != source)
        def _():
            arrival(source).wait_recv()

    @pl.loop(1, n_dev)
    def _(step):
        block_copy(step).wait_send()

    @pl.when(has_trail)
    def _():
        @pl.loop(1, n_dev)
        def _(step):
            trail_copy(step).wait_send()


def exchange_and_factor(numbers, points, scales, n_row, n_col):
    rows_one = points.shape[0]
    n_dev = n_row * n_col
    n_panel = 2 * PANEL // rows_one
    n_trail = SLAB // rows_one - n_panel
    strips_one = rows_one // (BLK * n_col)
    piece = (rows_one // n_row // 2, 2 * FEAT)
    strip = (BLK // 2, 2 * FEAT)
    n_own = n_trail * strips_one * BLK
    vmem = pl.BlockSpec(memory_space=pltpu.VMEM)
    shape = jax.ShapeDtypeStruct
    return pl.pallas_call(
        functools.partial(factor_kernel, n_row, n_col, n_panel, n_trail),
        out_shape=(
            shape((n_dev, *piece), jnp.float32),
            shape((n_panel, n_row, *piece), jnp.float32),
            shape((n_trail, strips_one, *strip), jnp.float32),
            shape((PANEL, PANEL), jnp.float32),
            shape((PANEL, PANEL), jnp.float32),
            shape((PANEL, PANEL), jnp.bfloat16),
            shape((n_own, 2 * PANEL), jnp.bfloat16),
        ),
        in_specs=[pl.BlockSpec(memory_space=pltpu.SMEM), vmem, vmem],
        out_specs=(vmem,) * 7,
        scratch_shapes=[
            pltpu.VMEM((n_row, *piece), jnp.float32),
            pltpu.VMEM((strips_one, n_col, *strip), jnp.float32),
            pltpu.VMEM((PANEL, PANEL), jnp.float32),
            pltpu.VMEM((PANEL, PANEL), jnp.float32),
            pltpu.SemaphoreType.DMA((n_dev,)),
            pltpu.SemaphoreType.DMA((n_dev,)),
            pltpu.SemaphoreType.DMA((n_dev,)),
            pltpu.SemaphoreType.DMA((n_trail,)),
            pltpu.SemaphoreType.DMA((n_panel, n_row)),
            pltpu.SemaphoreType.DMA((n_panel, n_row)),
            pltpu.SemaphoreType.DMA((1,)),
        ],
        compiler_params=pltpu.CompilerParams(
            collective_id=0, has_side_effects=True, vmem_limit_bytes=40 * 1024 * 1024
        ),
    )(numbers, points, scales)


def base_inverse(block):
    row = lax.broadcasted_iota(jnp.int32, (BASE, BASE), 0)
    col = lax.broadcasted_iota(jnp.int32, (BASE, BASE), 1)
    both = jnp.concatenate([block, (row == col).astype(jnp.float32)], axis=1)
    groups = BASE // SUB
    done = []
    for g in range(groups):
        height = BASE - SUB * g
        shape = (height, 2 * BASE)
        inside = lax.broadcasted_iota(jnp.int32, shape, 0)
        cols = [jnp.broadcast_to(both[:, SUB * g + j : SUB * g + j + 1], shape) for j in range(SUB)]
        scale = jnp.zeros((SUB, BASE), jnp.float32)
        for j in range(SUB):
            pivot = cols[j][j : j + 1]
            inverse = 1.0 / pivot
            scale = jnp.where(inside[:SUB, :BASE] == j, lax.rsqrt(pivot[:, :BASE]), scale)
            factors = jnp.where(inside > j, cols[j], 0.0)
            for k in range(j + 1, SUB):
                cols[k] = cols[k] - factors * (cols[j][k : k + 1] * inverse)
            both = both - factors * (both[j : j + 1] * inverse)
        done.append(both[:SUB, BASE:] * scale)
        both = both[SUB:]
    return jnp.concatenate(done, axis=0)


def full_dot(a, b, dims=((1,), (0,))):
    return lax.dot_general(
        a, b, (dims, ((), ())), precision=HIGHEST, preferred_element_type=jnp.float32
    )


def plain_dot(a, b, dims=((1,), (0,))):
    return lax.dot_general(a, b, (dims, ((), ())), preferred_element_type=jnp.float32)


def inverse_factor(a, out_ref, work_a, work_x):
    work_a[...] = (a + a.T) * 0.5
    row = lax.broadcasted_iota(jnp.int32, (PANEL, PANEL), 0)
    col = lax.broadcasted_iota(jnp.int32, (PANEL, PANEL), 1)
    work_x[...] = (row == col).astype(jnp.float32)
    out_ref[...] = jnp.zeros((PANEL, PANEL), jnp.float32)
    for start in range(0, PANEL, BASE):
        stop = start + BASE
        first = start // 128 * 128
        last = (stop + 127) // 128 * 128
        inverse = base_inverse(work_a[start:stop, start:stop])
        solved_x = joined_dot(inverse, work_x[start:stop, :last], ((1,), (0,)))
        out_ref[start:stop, :last] = solved_x
        if stop == PANEL:
            break
        solved_a = joined_dot(inverse, work_a[start:stop, first:], ((1,), (0,)))
        below = joined_dot(work_a[stop:, start:stop], inverse, ((1,), (1,)))
        kept = stop // 128 * 128
        work_a[stop:, kept:] -= joined_dot(below, solved_a[:, kept - first :], ((1,), (0,)))
        work_x[stop:, :last] -= joined_dot(below, solved_x, ((1,), (0,)))


def slab_kernel(
    n_row, n_col, block_rows,
    numbers, position, panel_ref, trail_ref, scales, one_ref, two_ref, second_ref, table_ref, rows_ref,
    out_ref, chosen_ref,
):
    signal = numbers[0]
    jitter = numbers[1]
    process_row = position[0]
    column = position[1]
    scale = scales[...]

    @pl.when(pl.program_id(0) == 0)
    def _():
        chosen_ref[: 2 * PANEL] = unpack(panel_ref[...]).reshape(2 * PANEL, FEAT) * scale
        chosen_ref[2 * PANEL :] = unpack(trail_ref[...]).reshape(-1, FEAT) * scale

    chunk = rows_ref.shape[0] * block_rows
    points = unpack(rows_ref[...]).reshape(chunk, FEAT) * scale
    group = BLK * n_col
    blocks = PANEL // group
    n_own = trail_ref.shape[0] * trail_ref.shape[1] * BLK

    def place(shape, axis):
        at = pl.program_id(0) * chunk + lax.broadcasted_iota(jnp.int32, shape, axis)
        return (at // block_rows * n_row + process_row) * block_rows + at % block_rows

    kernel = gaussian(points, chosen_ref[: 2 * PANEL], signal)
    col = lax.broadcasted_iota(jnp.int32, (1, 2 * PANEL), 1)
    kernel = kernel + jnp.where(place((chunk, 1), 0) == col, jitter, 0.0)
    owned = gaussian(chosen_ref[2 * PANEL :], points, signal)
    extra = lax.broadcasted_iota(jnp.int32, (n_own, 1), 0)
    col = 2 * PANEL + extra // BLK * group + column * BLK + extra % BLK
    owned = owned + jnp.where(place((1, chunk), 1) == col, jitter, 0.0)
    across = ((1,), (1,))
    first = full_dot(kernel[:, :PANEL], one_ref[...], across).astype(jnp.bfloat16)
    reduced = kernel[:, PANEL:] - plain_dot(first, second_ref[...], across)
    second = full_dot(reduced, two_ref[...], across).astype(jnp.bfloat16)
    trailing = owned - (
        plain_dot(table_ref[:, :PANEL], first, across) + plain_dot(table_ref[:, PANEL:], second, across)
    )
    line = lax.broadcasted_iota(jnp.int32, (blocks * BLK, PANEL), 0)
    wanted = line // BLK * group + column * BLK + line % BLK
    chosen = (lax.broadcasted_iota(jnp.int32, line.shape, 1) == wanted).astype(jnp.float32)
    chosen = chosen.astype(jnp.bfloat16)
    half = blocks * BLK
    out_ref[:half] = plain_dot(chosen, first, across).reshape(half, 1, chunk)
    out_ref[half : 2 * half] = plain_dot(chosen, second, across).reshape(half, 1, chunk)
    out_ref[2 * half :] = trailing.reshape(n_own, 1, chunk)


def slab(numbers, position, factored, scales, n_row, n_col, block_rows):
    rows, panel, trail, one, two, second, table = factored
    n_dev = n_row * n_col
    together = 512 // block_rows
    chunk = together * block_rows
    n_own = table.shape[0]
    n_out = n_own + 2 * PANEL // n_col
    vmem = pl.BlockSpec(memory_space=pltpu.VMEM)
    smem = pl.BlockSpec(memory_space=pltpu.SMEM)
    return pl.pallas_call(
        functools.partial(slab_kernel, n_row, n_col, block_rows),
        grid=(n_dev // together,),
        out_shape=jax.ShapeDtypeStruct((n_out, 1, n_dev * block_rows), jnp.float32),
        in_specs=[smem, smem] + [vmem] * 7
        + [pl.BlockSpec((together, *rows.shape[1:]), lambda i: (i, 0, 0))],
        out_specs=pl.BlockSpec((n_out, 1, chunk), lambda i: (0, 0, i)),
        scratch_shapes=[
            pltpu.VMEM((2 * PANEL + n_own, FEAT), jnp.float32),
        ],
        compiler_params=pltpu.CompilerParams(vmem_limit_bytes=40 * 1024 * 1024),
    )(numbers, position, panel, trail, scales, one, two, second, table, rows)


def on_device(points, feature_scales, amplitude, ridge):
    n_row = lax.axis_size("row")
    n_col = lax.axis_size("col")
    block_rows = points.shape[0] // n_row
    numbers = jnp.concatenate([amplitude, ridge])
    position = jnp.stack([lax.axis_index("row"), lax.axis_index("col")]).astype(jnp.int32)
    scales = feature_scales[None]
    factored = exchange_and_factor(numbers, points, scales, n_row, n_col)
    finished = slab(numbers, position, factored, scales, n_row, n_col, block_rows)
    return finished.reshape(SLAB // (BLK * n_col), 1, BLK, 1, -1)


def solution(mesh):
    placed = (P(("row", "col"), None), P(), P(), P())
    return jax.shard_map(
        on_device,
        mesh=mesh,
        in_specs=placed,
        out_specs=P(None, "col", None, "row", None),
        check_vma=False,
    )
```
